32 devices in a mesh: groups: 2 (over x), seq: 8 (over z, y), tensor: 2 (over core).
Axes of the slice: x: 2, y: 2, z: 4, core: 2. Of those that a mesh axis runs over, the one named last changes fastest.
Arguments:
- queries: bfloat16 [2048, 4096], P(('groups', 'seq'), 'tensor'), parts along dimension 0, may hold values from -80 to 80
- resp_keys: bfloat16 [2048, 512], P(('groups', 'seq'), 'tensor'), parts along dimension 0, may hold values from -18 to 18
- resp_values: bfloat16 [2048, 512], P(('groups', 'seq'), 'tensor'), parts along dimension 0, may hold values from -24 to 24
- prompt_keys: bfloat16 [16384, 512], P(('groups', 'seq'), 'tensor'), parts along dimension 0, may hold values from -12 to 12
- prompt_values: bfloat16 [16384, 512], P(('groups', 'seq'), 'tensor'), parts along dimension 0, may hold values from -24 to 24
- response_prompt: int32 [64, 1], P(('groups', 'seq')), parts along dimension 0, may hold values from 0 to 3; in each aligned block of 4 rows (0 to 3, 4 to 7, ...) no two rows name the same one
- response_lengths: int32 [16, 4], P(('groups', 'seq')), parts along dimension 0, may hold values from 1 to 40, 128 in all within a row
- shard_order: int32 [16], P('groups'), parts along dimension 0, may hold values from 0 to 7, each once
Outputs:
- attended: bfloat16 [2048, 4096], P(('groups', 'seq'), 'tensor'), parts along dimension 0
The draws below stay inside these ranges and needn't reach their ends.
There are 2 independent parts, one for each index of `groups`. The reference program is written for one: setup_inputs(seed, part) draws one part's arguments, and reference() takes and returns one part's arrays. A program takes and returns all parts, laid end to end along the dimension named above; each array names one. Nothing has to cross between parts.
Inputs may be any that keep to these rules, and one draw needn't show every extreme that they name: `response_prompt`: the responses of one pack belong to different prompts. `response_lengths`: the lengths of one pack add up to 128; the longest response of every pack has 40 tokens. `shard_order`: A permutation of 0 .. 7.
All inputs are finite; a program needn't handle non-finite values.
Results may differ from the reference program's by a relative error of at most 0.0056.
Values may be sent and summed in bfloat16 or wider, within the bound.
A program may use at most 64 MiB of HBM per device.

```python
import math
import jax
import jax.numpy as jnp
import numpy as np
from jax import lax

QH = 32
KVH = 4
HD = 128
TOK_DEV = 128
KV_DEV = 1024
RESP_DEV = 4
PROMPTS = 4
SHARDS = 2
LEN_MOST = 40
RESPONSES = 32
TOKENS = 1024
KV_TOKENS = 8192
N_SEQ = 8


def key_source(key):
    drawn_draw = 3.0 * jax.random.normal(jax.random.fold_in(key, 11), (TOKENS, KVH * HD), jnp.float32)
    return jnp.clip(drawn_draw, -18.0, 18.0)


def draw_resp_keys(key, part):
    keys_drawn = key_source(key)
    return keys_drawn.astype(jnp.bfloat16)


def draw_queries(key, part):
    drawn = jnp.clip(jax.random.normal(jax.random.fold_in(key, 12), (TOKENS, QH * HD), jnp.float32), -6.0, 6.0)
    return drawn.astype(jnp.bfloat16)


def level_of(own_key, dims, pieces, least, largest):
    def one(position, blocks):
        draws = jax.random.uniform(jax.random.fold_in(jax.random.fold_in(own_key, 6), position), (blocks,), jnp.float32, least / len(pieces), largest / len(pieces))
        return jnp.repeat(jnp.exp(draws), dims[position] // blocks).reshape((-1,) + (1,) * (len(dims) - position - 1))

    factor_of = one(*pieces[0])
    for cut in pieces[1:]:
        factor_of = factor_of * one(*cut)
    return factor_of


def split_up(amount, total, bound, lean):
    weights = [(1 << 20) // math.isqrt(grade ** lean) + 1 for grade in range(2, amount + 1)]
    rest, given = total - bound - (amount - 1), [1] * (amount - 1)
    while rest > 0:
        candidates = [i for i in range(amount - 1) if given[i] < bound]
        whole, remaining = sum([weights[i] for i in candidates]), rest
        for i in candidates:
            addition = min(bound - given[i], max(1, remaining * weights[i] // whole), rest)
            given[i] = given[i] + addition
            rest = rest - addition
    return np.array([bound] + given)


def uneven_parts(own_key, count, total, reach, slope):
    if count == 2:
        one = jax.random.randint(own_key, (), max(1, total - reach), min(reach, total - 1) + 1)
        return jnp.stack([one, total - one])
    sizes = jnp.asarray(split_up(count, total, reach, slope), jnp.int32)
    pairs = (count - 1) // 2
    giver, taker = sizes[1:1 + 2 * pairs:2], sizes[2:2 + 2 * pairs:2]
    slack = jnp.minimum(giver - 1, reach - taker)
    passed = jax.random.randint(jax.random.fold_in(own_key, 1), (pairs,), 0, 1 << 20) % (slack + 1)
    sizes = sizes.at[1:1 + 2 * pairs:2].set(giver - passed).at[2:2 + 2 * pairs:2].set(taker + passed)
    return sizes[jax.random.permutation(jax.random.fold_in(own_key, 2), count)]


def deal_out(rng, own, number, rows, count, top, most, lean):
    ranking = jax.random.permutation(rng, count)
    heavy_load, common = load_shares(count, rows * top, most, lean, True), load_shares(count, rows * top, most, lean, False)
    places = jnp.arange(count)

    def named(tallies, offset_by):
        used = int((tallies > 0).sum())
        fixed = max(1, used // 4)
        moved = fixed + (places - fixed + offset_by * (used - fixed)) % max(1, count - fixed)
        return jnp.zeros((count,), jnp.int32).at[ranking[jnp.where(places < fixed, places, moved)]].set(jnp.asarray(tallies, jnp.int32))

    tallies = jnp.where(number % 4 == 0, named(heavy_load, number // 4), named(common, number - number // 4 - 1))
    mixed = jax.random.permutation(jax.random.fold_in(own, 3), count)
    source_of, receiver = mixed[0:count // 2 * 2:2], mixed[1:count // 2 * 2:2]
    margin = jnp.minimum(tallies[source_of] - 1, most - tallies[receiver]) // 2
    margin = jnp.where((source_of == ranking[0]) | (receiver == ranking[0]) | (tallies[receiver] == 0), 0, jnp.maximum(margin, 0))
    moved = jax.random.randint(jax.random.fold_in(own, 4), (count // 2,), 0, 1 << 20) % (margin + 1)
    tallies = tallies.at[source_of].add(-moved).at[receiver].add(moved)
    labels = jnp.searchsorted(jnp.cumsum(tallies), jnp.arange(rows * top), side="right").astype(jnp.int32)
    grid = labels.reshape(top, rows).T
    grid = grid[jax.random.permutation(jax.random.fold_in(own, 1), rows)]
    offset_by = jax.random.randint(jax.random.fold_in(own, 2), (rows, 1), 0, top)
    return jnp.take_along_axis(grid, (jnp.arange(top)[None, :] + offset_by) % top, axis=1)


def load_shares(count, total, reach, lean, full):
    portions = [(1 << 20) // math.isqrt(standing ** lean) + 1 for standing in range(1, count + 1)]
    largest = reach if full else min(reach, max(-(-total // count), total * portions[0] // sum(portions)))
    least = 1 if total - largest >= count - 1 else 0
    given, surplus = [largest] + [least] * (count - 1), total - largest - least * (count - 1)
    while surplus > 0:
        free = [i for i in range(1, count) if given[i] < largest] or [i for i in range(1, count) if given[i] < reach]
        pool, budget = sum([portions[i] for i in free]), surplus
        for i in free:
            addition = min(reach - given[i], max(1, budget * portions[i] // pool), surplus)
            given[i] = given[i] + addition
            surplus = surplus - addition
    return np.array(given)


def bell_draw(rng, extent, width, most, pieces=(), kind=jnp.bfloat16):
    entries = jax.random.normal(rng, extent, jnp.float32) * width
    if len(pieces) > 0:
        entries = level_of(rng, extent, pieces, -0.22, 0.18) * entries
    return jnp.clip(entries, min=-most, max=most).astype(kind)


def setup_inputs(seed: int = 0, part: int = 0) -> dict:
    seeds = jax.random.split(jax.random.key(seed), 9)
    part_keys = jax.random.split(jax.random.fold_in(seeds[8], part), 9)
    queries = draw_queries(jax.random.fold_in(jax.random.fold_in(seeds[8], part), 71), part)
    resp_keys = draw_resp_keys(jax.random.fold_in(jax.random.fold_in(seeds[8], part), 71), part)
    resp_values = bell_draw(part_keys[2], (TOKENS, KVH * HD), 4.0, 24.0, ((0, 8), (1, 2)))
    prompt_keys = bell_draw(part_keys[3], (KV_TOKENS, KVH * HD), 2.0, 12.0, ((0, 8), (1, 2)))
    prompt_values = bell_draw(part_keys[4], (KV_TOKENS, KVH * HD), 4.0, 24.0, ((0, 8), (1, 2)))
    response_prompt_keys = jax.random.split(jax.random.fold_in(part_keys[5], 1), RESPONSES // RESP_DEV)
    response_prompt_turns = jax.random.permutation(jax.random.fold_in(part_keys[5], 3), RESPONSES // RESP_DEV)
    response_prompt = jax.vmap(lambda own, number: deal_out(jax.random.fold_in(part_keys[5], 2), own, number, RESP_DEV, PROMPTS, 1, 1, 2))(response_prompt_keys, response_prompt_turns).reshape((RESPONSES, 1))
    response_lengths = jax.vmap(lambda own: uneven_parts(own, RESP_DEV, TOK_DEV, LEN_MOST, 2))(jax.random.split(part_keys[6], N_SEQ)).reshape((N_SEQ, RESP_DEV)).astype(jnp.int32)
    shard_order = jax.random.permutation(part_keys[7], N_SEQ).astype(jnp.int32)
    return dict(queries=queries, resp_keys=resp_keys, resp_values=resp_values, prompt_keys=prompt_keys, prompt_values=prompt_values, response_prompt=response_prompt, response_lengths=response_lengths, shard_order=shard_order)


def attend(rows, keys, values, key_heads, head_dim, allowed):
    row_count = rows.shape[0]
    head_count = rows.shape[1] // head_dim
    grouping = head_count // key_heads
    scaling = 1.0 / math.sqrt(head_dim)
    results = []
    log_parts = []
    for kv_index in range(key_heads):
        query_rows = rows[:, kv_index * grouping * head_dim:(kv_index + 1) * grouping * head_dim]
        query_rows = query_rows.reshape(row_count * grouping, head_dim)
        key_part = keys[:, kv_index * head_dim:(kv_index + 1) * head_dim]
        value_part = values[:, kv_index * head_dim:(kv_index + 1) * head_dim]
        scores = lax.dot_general(query_rows, key_part, (((1,), (1,)), ((), ())), preferred_element_type=jnp.float32) * scaling
        if allowed is not None:
            scores = jnp.where(jnp.repeat(allowed, grouping, axis=0), scores, -1e+30)
        highest = lax.optimization_barrier(jnp.max(scores, axis=1, keepdims=True))
        summed = lax.optimization_barrier(jnp.sum(jnp.exp(scores - highest), axis=1, keepdims=True))
        log_total = highest + jnp.log(summed)
        weights = jnp.exp(scores - log_total).astype(jnp.bfloat16)
        result = jnp.dot(weights, value_part, preferred_element_type=jnp.float32)
        results.append(result.reshape(row_count, grouping * head_dim))
        log_parts.append(log_total.reshape(row_count, grouping))
    return (jnp.concatenate(results, axis=1), jnp.concatenate(log_parts, axis=1))

def combine(parts_out, parts_log, head_dim):
    stacked = jnp.stack(parts_log)
    highest = lax.optimization_barrier(jnp.max(stacked, axis=0))
    total_log = highest + jnp.log(lax.optimization_barrier(jnp.sum(jnp.exp(stacked - highest), axis=0)))
    row_count, head_count = total_log.shape
    blended = jnp.zeros((row_count, head_count, head_dim), jnp.float32)
    for result, log_part in zip(parts_out, parts_log):
        blended = blended + jnp.exp(log_part - total_log)[:, :, None] * result.reshape(row_count, head_count, head_dim)
    return blended.reshape(row_count, head_count * head_dim).astype(jnp.bfloat16)

def reference(queries, resp_keys, resp_values, prompt_keys, prompt_values, response_prompt, response_lengths, shard_order):
    device_ids = jnp.arange(N_SEQ, dtype=jnp.int32)
    inverse = lax.optimization_barrier(jnp.sum(jnp.where(shard_order[None, :] == device_ids[:, None], device_ids[None, :], 0), axis=1)).astype(jnp.int32)
    query_blocks = queries.reshape(N_SEQ, TOK_DEV, QH * HD)
    key_blocks = resp_keys.reshape(N_SEQ, TOK_DEV, KVH * HD)
    value_blocks = resp_values.reshape(N_SEQ, TOK_DEV, KVH * HD)
    prompt_blocks = response_prompt.reshape(N_SEQ, RESP_DEV)

    def per_pack(inputs):
        query_rows, pack_keys, pack_values, prompts, lengths = inputs
        finish = jnp.cumsum(lengths).astype(jnp.int32)
        starts = (finish - lengths).astype(jnp.int32)
        token_ids = jnp.arange(TOK_DEV, dtype=jnp.int32)
        segment = (lax.optimization_barrier(jnp.sum((token_ids[:, None] >= starts[None, :]).astype(jnp.int32), axis=1)) - 1).astype(jnp.int32)
        offset = (token_ids - jnp.take(starts, segment)).astype(jnp.int32)
        allowed = (segment[:, None] == segment[None, :]) & (token_ids[None, :] <= token_ids[:, None])
        local_out, local_log = attend(query_rows, pack_keys, pack_values, KVH, HD, allowed)
        padded = jnp.concatenate([query_rows, jnp.zeros((LEN_MOST, QH * HD), query_rows.dtype)], axis=0)
        parts_out = [local_out]
        parts_log = [local_log]
        for shard_rank in range(SHARDS):
            window_out = []
            window_log = []
            for resp_rank in range(RESP_DEV):
                owner_dev = jnp.take(inverse, prompts[resp_rank] * SHARDS + shard_rank).astype(jnp.int32)
                first_row = (owner_dev * KV_DEV).astype(jnp.int32)
                shard_keys = lax.dynamic_slice_in_dim(prompt_keys, first_row, KV_DEV, 0)
                shard_values = lax.dynamic_slice_in_dim(prompt_values, first_row, KV_DEV, 0)
                window = lax.dynamic_slice_in_dim(padded, starts[resp_rank].astype(jnp.int32), LEN_MOST, 0)
                result, log_part = attend(window, shard_keys, shard_values, KVH, HD, None)
                window_out.append(result.astype(jnp.bfloat16))
                window_log.append(log_part)
            all_out = jnp.concatenate(window_out, axis=0)
            all_log = jnp.concatenate(window_log, axis=0)
            flat_index = (segment * LEN_MOST + offset).astype(jnp.int32)
            parts_out.append(jnp.take(all_out, flat_index, axis=0).astype(jnp.float32))
            parts_log.append(jnp.take(all_log, flat_index, axis=0))
        return combine(parts_out, parts_log, HD)
    blended = lax.map(per_pack, (query_blocks, key_blocks, value_blocks, prompt_blocks, response_lengths))
    return blended.reshape(TOKENS, QH * HD)
```

```python
import functools
import math

import jax
import jax.numpy as jnp
from jax import lax
from jax.experimental import pallas as pl
from jax.experimental.pallas import tpu as pltpu
from jax.sharding import PartitionSpec as P

HD = 128
PROMPTS = 4
LEN_MOST = 40
LANES = 128
GROUPS_OF_8 = LEN_MOST // 8
LOG2E = 1.4426950408889634
MESH = pl.DeviceIdType.MESH

F32 = jnp.float32
BF16 = jnp.bfloat16


def xor(a, b, n):
    total = 0
    bit = 1
    while bit < n:
        total = total + bit * (((a // bit) % 2 + (b // bit) % 2) % 2)
        bit *= 2
    return total


def nt_dot(a, b):
    return lax.dot_general(a, b, (((1,), (1,)), ((), ())), preferred_element_type=F32)


def kernel(
    n,
    order_ref,
    prompt_ref,
    len_ref,
    q_ref,
    rk_ref,
    rv_ref,
    pk_ref,
    pv_ref,
    out_ref,
    send_q,
    recv_q,
    send_o,
    recv_o,
    send_l,
    recv_l,
    v_ext,
    rv_ext,
    local_o,
    local_l,
    q_send_sem,
    q_recv_sem,
    o_send_sem,
    o_recv_sem,
    l_send_sem,
    l_recv_sem,
):
    me = lax.axis_index("seq")
    shards = n // PROMPTS
    tok = q_ref.shape[0]
    kv_heads = rk_ref.shape[1] // HD
    heads = q_ref.shape[1] // HD
    per_kv = heads // kv_heads
    rows = per_kv * LEN_MOST
    resp = prompt_ref.shape[0]
    power = LOG2E / math.sqrt(HD)

    def peer_of(step):
        return xor(me, step, n) if n & (n - 1) == 0 else lax.rem(me + step, n)

    def giver_of(step):
        return xor(me, step, n) if n & (n - 1) == 0 else lax.rem(me + n - step, n)

    barrier = pltpu.get_barrier_semaphore()

    def greet(step, carry):
        pl.semaphore_signal(
            barrier, inc=1, device_id={"seq": peer_of(step)}, device_id_type=MESH
        )
        return carry

    lax.fori_loop(1, n, greet, 0)

    lengths = [len_ref[0, k] for k in range(resp)]
    prompts = [prompt_ref[k, 0] for k in range(resp)]
    starts = [jnp.int32(0)]
    for k in range(resp - 1):
        starts.append(starts[-1] + lengths[k])

    def placed(d):
        rank = order_ref[d]
        first = jnp.int32(0)
        live = jnp.int32(0)
        which = jnp.int32(0)
        for k in range(resp):
            low = prompts[k] * shards
            hit = (rank >= low) & (rank < low + shards)
            first = jnp.where(hit, starts[k], first)
            live = jnp.where(hit, lengths[k], live)
            which = jnp.where(hit, rank - low, which)
        return first, live, which

    slot = lax.broadcasted_iota(jnp.int32, (LEN_MOST, tok), 0)
    token = lax.broadcasted_iota(jnp.int32, (LEN_MOST, tok), 1)

    def gather_block(d):
        first, live, _ = placed(d)
        chosen = ((token == first + slot) & (slot < live)).astype(F32).astype(BF16)
        picked = jnp.dot(chosen, q_ref[...], preferred_element_type=F32)
        for g in range(kv_heads):
            parts = [
                picked[:, (g * per_kv + h) * HD : (g * per_kv + h + 1) * HD] for h in range(per_kv)
            ]
            send_q[d, g] = jnp.concatenate(parts, axis=0).astype(BF16)

    def q_copy(slot_from, slot_to, peer):
        return pltpu.make_async_remote_copy(
            src_ref=send_q.at[slot_from],
            dst_ref=recv_q.at[slot_to],
            send_sem=q_send_sem.at[slot_from],
            recv_sem=q_recv_sem.at[slot_to],
            device_id={"seq": peer},
            device_id_type=MESH,
        )

    def o_copy(slot_from, slot_to, peer):
        return pltpu.make_async_remote_copy(
            src_ref=send_o.at[slot_from],
            dst_ref=recv_o.at[slot_to],
            send_sem=o_send_sem.at[slot_from],
            recv_sem=o_recv_sem.at[slot_to],
            device_id={"seq": peer},
            device_id_type=MESH,
        )

    def l_copy(slot_from, slot_to, peer):
        return pltpu.make_async_remote_copy(
            src_ref=send_l.at[slot_from],
            dst_ref=recv_l.at[slot_to],
            send_sem=l_send_sem.at[slot_from],
            recv_sem=l_recv_sem.at[slot_to],
            device_id={"seq": peer},
            device_id_type=MESH,
        )

    pl.semaphore_wait(barrier, n - 1)

    def send_step(i, carry):
        peer = peer_of(n - 1 - i)
        gather_block(peer)
        q_copy(peer, me, peer).start()
        return carry

    lax.fori_loop(0, n - 1, send_step, 0)
    gather_block(me)

    ones = jnp.ones((pk_ref.shape[0], HD), BF16)
    for g in range(kv_heads):
        v_ext[g] = jnp.concatenate([pv_ref[:, g * HD : (g + 1) * HD], ones], axis=1)
    ones = jnp.ones((tok, HD), BF16)
    for g in range(kv_heads):
        rv_ext[g] = jnp.concatenate([rv_ref[:, g * HD : (g + 1) * HD], ones], axis=1)

    lane8 = lax.broadcasted_iota(jnp.int32, (8, LANES), 1)

    def owner_block(q_block, g):
        scores = nt_dot(q_block, pk_ref[:, g * HD : (g + 1) * HD])
        highest = jnp.max(scores, axis=1, keepdims=True)
        weights = jnp.exp2((scores - highest) * power).astype(BF16)
        both = jnp.dot(weights, v_ext[g], preferred_element_type=F32)
        total = both[:, HD:]
        return (both[:, :HD] / total).astype(BF16), highest * power + jnp.log2(total)

    def packed_logs(logs):
        packed = jnp.zeros((8, LANES), F32)
        for g in range(kv_heads):
            for h in range(per_kv):
                for k in range(GROUPS_OF_8):
                    row = h * LEN_MOST + k * 8
                    packed = jnp.where(
                        lane8 == k * heads + g * per_kv + h, logs[g][row : row + 8, :], packed
                    )
        return packed

    def own_block():
        logs = []
        for g in range(kv_heads):
            result, log_part = owner_block(send_q[me, g], g)
            recv_o[me, g] = result
            logs.append(log_part)
        recv_l[me] = packed_logs(logs)

    def serve(step, carry):
        peer = giver_of(step)
        q_copy(peer, peer, peer).wait_recv()
        logs = []
        for g in range(kv_heads):
            result, log_part = owner_block(recv_q[peer, g], g)
            send_o[peer, g] = result
            logs.append(log_part)
        send_l[peer] = packed_logs(logs)
        o_copy(peer, me, peer).start()
        l_copy(peer, me, peer).start()
        return carry

    own_block()

    row_id = lax.broadcasted_iota(jnp.int32, (tok, tok), 0)
    col_id = lax.broadcasted_iota(jnp.int32, (tok, tok), 1)
    begin = jnp.zeros((tok, tok), jnp.int32)
    for k in range(1, resp):
        begin = jnp.where(row_id >= starts[k], starts[k], begin)
    allowed = (col_id >= begin) & (col_id <= row_id)
    lane_tok = lax.broadcasted_iota(jnp.int32, (tok, LANES), 1)

    local_log = jnp.zeros((tok, LANES), F32)
    for h in range(heads):
        g = h // per_kv
        scores = nt_dot(q_ref[:, h * HD : (h + 1) * HD], rk_ref[:, g * HD : (g + 1) * HD])
        scores = jnp.where(allowed, scores, -1e30)
        highest = jnp.max(scores, axis=1, keepdims=True)
        weights = jnp.exp2((scores - highest) * power).astype(BF16)
        both = jnp.dot(weights, rv_ext[g], preferred_element_type=F32)
        total = both[:, HD:]
        local_o[h] = both[:, :HD] / total
        local_log = jnp.where(lane_tok == h, highest * power + jnp.log2(total), local_log)
    local_l[...] = local_log

    lax.fori_loop(1, n, serve, 0)

    column = lax.broadcasted_iota(jnp.int32, (8, n * LEN_MOST), 1)
    targets = [jnp.full((8, n * LEN_MOST), -1, jnp.int32) for _ in range(shards)]
    for d in range(n):
        first, live, which = placed(d)
        place = column - d * LEN_MOST
        here = (place >= 0) & (place < live)
        for j in range(shards):
            targets[j] = jnp.where(here & (which == j), place + first, targets[j])
    token_row = lax.broadcasted_iota(jnp.int32, (tok, n * LEN_MOST), 0)
    chosen = [
        (token_row == jnp.broadcast_to(t[0:1, :], (tok, n * LEN_MOST))).astype(F32).astype(BF16)
        for t in targets
    ]
    chosen = jnp.concatenate(chosen, axis=0)

    def receive(step, carry):
        peer = giver_of(step)
        o_copy(peer, peer, peer).wait_recv()
        l_copy(peer, peer, peer).wait_recv()
        return carry

    lax.fori_loop(1, n, receive, 0)

    log_rows = []
    for d in range(n):
        packed = recv_l[d]
        for k in range(GROUPS_OF_8):
            log_rows.append(pltpu.roll(packed, LANES - k * heads, 1) if k else packed)
    log_all = jnp.concatenate(log_rows, axis=0)
    high = log_all.astype(BF16)
    rest = log_all - high.astype(F32)
    middle = rest.astype(BF16)
    low = (rest - middle.astype(F32)).astype(BF16)
    logs = jnp.dot(chosen, high, preferred_element_type=F32)
    logs = logs + jnp.dot(chosen, middle, preferred_element_type=F32)
    logs = logs + jnp.dot(chosen, low, preferred_element_type=F32)
    parts_log = [local_l[...]] + [logs[j * tok : (j + 1) * tok] for j in range(shards)]
    highest = functools.reduce(jnp.maximum, parts_log)
    shares = [jnp.exp2(part - highest) for part in parts_log]
    inverse = 1.0 / functools.reduce(jnp.add, shares)
    shares = [share * inverse for share in shares]

    for g in range(kv_heads):
        wide = [recv_o[d, g].astype(F32) for d in range(n)]
        for h in range(per_kv):
            head = g * per_kv + h
            stacked = jnp.concatenate(
                [w[h * LEN_MOST : (h + 1) * LEN_MOST] for w in wide], axis=0
            ).astype(BF16)
            taken = jnp.dot(chosen, stacked, preferred_element_type=F32)
            blended = shares[0][:, head : head + 1] * local_o[head]
            for j in range(shards):
                blended = blended + (
                    shares[j + 1][:, head : head + 1] * taken[j * tok : (j + 1) * tok]
                )
            out_ref[:, head * HD : (head + 1) * HD] = blended.astype(BF16)

    def finish(step, carry):
        peer = peer_of(step)
        q_copy(peer, me, peer).wait_send()
        o_copy(peer, me, peer).wait_send()
        l_copy(peer, me, peer).wait_send()
        return carry

    lax.fori_loop(1, n, finish, 0)


def per_device(
    queries,
    resp_keys,
    resp_values,
    prompt_keys,
    prompt_values,
    response_prompt,
    response_lengths,
    shard_order,
):
    n = lax.axis_size("seq")
    tok = queries.shape[0]
    kv_heads = resp_keys.shape[1] // HD
    heads = queries.shape[1] // HD
    rows = heads // kv_heads * LEN_MOST
    keys = prompt_keys.shape[0]
    block = (n, kv_heads, rows, HD)
    smem = pl.BlockSpec(memory_space=pltpu.SMEM)
    vmem = pl.BlockSpec(memory_space=pltpu.VMEM)
    return pl.pallas_call(
        functools.partial(kernel, n),
        out_shape=jax.ShapeDtypeStruct(queries.shape, BF16),
        in_specs=[smem] * 3 + [vmem] * 5,
        out_specs=vmem,
        scratch_shapes=[
            pltpu.VMEM(block, BF16),
            pltpu.VMEM(block, BF16),
            pltpu.VMEM(block, BF16),
            pltpu.VMEM(block, BF16),
            pltpu.VMEM((n, 8, LANES), F32),
            pltpu.VMEM((n, 8, LANES), F32),
            pltpu.VMEM((kv_heads, keys, 2 * HD), BF16),
            pltpu.VMEM((kv_heads, tok, 2 * HD), BF16),
            pltpu.VMEM((heads, tok, HD), F32),
            pltpu.VMEM((tok, LANES), F32),
        ]
        + [pltpu.SemaphoreType.DMA((n,))] * 6,
        compiler_params=pltpu.CompilerParams(
            collective_id=0, has_side_effects=True, vmem_limit_bytes=56 * 1024 * 1024
        ),
    )(
        shard_order,
        response_prompt,
        response_lengths,
        queries,
        resp_keys,
        resp_values,
        prompt_keys,
        prompt_values,
    )


def solution(mesh):
    return jax.shard_map(
        per_device,
        mesh=mesh,
        in_specs=(
            P(("groups", "seq"), "tensor"),
            P(("groups", "seq"), "tensor"),
            P(("groups", "seq"), "tensor"),
            P(("groups", "seq"), "tensor"),
            P(("groups", "seq"), "tensor"),
            P(("groups", "seq"), None),
            P(("groups", "seq"), None),
            P("groups"),
        ),
        out_specs=P(("groups", "seq"), "tensor"),
        check_vma=False,
    )
```

```python
import functools
import math

import jax
import jax.numpy as jnp
from jax import lax
from jax.experimental import pallas as pl
from jax.experimental.pallas import tpu as pltpu
from jax.sharding import PartitionSpec as P

HD = 128
PROMPTS = 4
LEN_MOST = 40
LANES = 128
GROUPS_OF_8 = LEN_MOST // 8
LOG2E = 1.4426950408889634
MESH = pl.DeviceIdType.MESH

F32 = jnp.float32
BF16 = jnp.bfloat16


def xor(a, b, n):
    total = 0
    bit = 1
    while bit < n:
        total = total + bit * (((a // bit) % 2 + (b // bit) % 2) % 2)
        bit *= 2
    return total


def nt_dot(a, b):
    return lax.dot_general(a, b, (((1,), (1,)), ((), ())), preferred_element_type=F32)


def kernel(
    n,
    order_ref,
    prompt_ref,
    len_ref,
    q_ref,
    rk_ref,
    rv_ref,
    pk_ref,
    pv_ref,
    out_ref,
    send_q,
    recv_q,
    send_o,
    recv_o,
    send_l,
    recv_l,
    far_kv,
    v_ext,
    rv_ext,
    local_o,
    local_l,
    q_send_sem,
    q_recv_sem,
    o_send_sem,
    o_recv_sem,
    l_send_sem,
    l_recv_sem,
    kv_send_sem,
    kv_recv_sem,
):
    me = lax.axis_index("seq")
    half = n // 2
    mate = xor(me, half, n)
    shards = n // PROMPTS
    tok = q_ref.shape[0]
    kv_heads = rk_ref.shape[1] // HD
    heads = q_ref.shape[1] // HD
    per_kv = heads // kv_heads
    resp = prompt_ref.shape[0]
    power = LOG2E / math.sqrt(HD)

    barrier = pltpu.get_barrier_semaphore()

    def greet(step, carry):
        pl.semaphore_signal(
            barrier, inc=1, device_id={"seq": xor(me, step, n)}, device_id_type=MESH
        )
        return carry

    lax.fori_loop(1, n, greet, 0)

    lengths = [len_ref[0, k] for k in range(resp)]
    prompts = [prompt_ref[k, 0] for k in range(resp)]
    starts = [jnp.int32(0)]
    for k in range(resp - 1):
        starts.append(starts[-1] + lengths[k])

    def placed(d):
        rank = order_ref[d]
        first = jnp.int32(0)
        live = jnp.int32(0)
        which = jnp.int32(0)
        for k in range(resp):
            low = prompts[k] * shards
            hit = (rank >= low) & (rank < low + shards)
            first = jnp.where(hit, starts[k], first)
            live = jnp.where(hit, lengths[k], live)
            which = jnp.where(hit, rank - low, which)
        return first, live, which

    slot_id = lax.broadcasted_iota(jnp.int32, (LEN_MOST, tok), 0)
    token_id = lax.broadcasted_iota(jnp.int32, (LEN_MOST, tok), 1)

    def gather_block(d):
        first, live, _ = placed(d)
        chosen = ((token_id == first + slot_id) & (slot_id < live)).astype(F32).astype(BF16)
        picked = jnp.dot(chosen, q_ref[...], preferred_element_type=F32)
        for g in range(kv_heads):
            parts = [
                picked[:, (g * per_kv + h) * HD : (g * per_kv + h + 1) * HD] for h in range(per_kv)
            ]
            send_q[d, g] = jnp.concatenate(parts, axis=0).astype(BF16)

    def q_copy(d, g, giver, slot, peer):
        return pltpu.make_async_remote_copy(
            src_ref=send_q.at[d, g],
            dst_ref=recv_q.at[giver, slot],
            send_sem=q_send_sem.at[d, g],
            recv_sem=q_recv_sem.at[giver, slot],
            device_id={"seq": peer},
            device_id_type=MESH,
        )

    def o_copy(giver, slot, d, g, peer):
        return pltpu.make_async_remote_copy(
            src_ref=send_o.at[giver, slot],
            dst_ref=recv_o.at[d, g],
            send_sem=o_send_sem.at[giver, slot],
            recv_sem=o_recv_sem.at[d, g],
            device_id={"seq": peer},
            device_id_type=MESH,
        )

    def l_copy(giver, slot, d, g, peer):
        return pltpu.make_async_remote_copy(
            src_ref=send_l.at[giver, slot],
            dst_ref=recv_l.at[d, g],
            send_sem=l_send_sem.at[giver, slot],
            recv_sem=l_recv_sem.at[d, g],
            device_id={"seq": peer},
            device_id_type=MESH,
        )

    def kv_copy(which):
        source = (pk_ref, pv_ref)[which]
        return pltpu.make_async_remote_copy(
            src_ref=source.at[:, pl.ds(HD, HD)],
            dst_ref=far_kv.at[which],
            send_sem=kv_send_sem.at[which],
            recv_sem=kv_recv_sem.at[which],
            device_id={"seq": mate},
            device_id_type=MESH,
        )

    pl.semaphore_wait(barrier, n - 1)

    def send_far(step, carry):
        peer = xor(me, step, n)
        gather_block(peer)
        q_copy(peer, 0, me, 0, peer).start()
        return carry

    def send_near(step, carry):
        peer = xor(me, step, n)
        gather_block(peer)
        q_copy(peer, 0, me, 0, peer).start()
        q_copy(peer, 1, me, 1, peer).start()
        q_copy(xor(peer, half, n), 1, me, 2, peer).start()
        return carry

    kv_copy(0).start()
    kv_copy(1).start()
    lax.fori_loop(half, n, send_far, 0)
    lax.fori_loop(1, half, send_near, 0)
    gather_block(me)

    ones = jnp.ones((pk_ref.shape[0], HD), BF16)
    for g in range(kv_heads):
        v_ext[g] = jnp.concatenate([pv_ref[:, g * HD : (g + 1) * HD], ones], axis=1)
    ones = jnp.ones((tok, HD), BF16)
    for g in range(kv_heads):
        rv_ext[g] = jnp.concatenate([rv_ref[:, g * HD : (g + 1) * HD], ones], axis=1)

    lane8 = lax.broadcasted_iota(jnp.int32, (8, LANES), 1)

    def owner_block(q_block, g, far=False):
        keys = far_kv[0] if far else pk_ref[:, g * HD : (g + 1) * HD]
        scores = nt_dot(q_block, keys)
        highest = jnp.max(scores, axis=1, keepdims=True)
        weights = jnp.exp2((scores - highest) * power).astype(BF16)
        both = jnp.dot(weights, v_ext[kv_heads if far else g], preferred_element_type=F32)
        total = both[:, HD:]
        logs = highest * power + jnp.log2(total)
        packed = jnp.zeros((8, LANES), F32)
        for h in range(per_kv):
            for k in range(GROUPS_OF_8):
                row = h * LEN_MOST + k * 8
                packed = jnp.where(
                    lane8 == k * heads + g * per_kv + h, logs[row : row + 8, :], packed
                )
        return (both[:, :HD] / total).astype(BF16), packed

    def serve(giver, slot):
        g = min(slot, 1)
        owner = mate if slot == 2 else me
        q_copy(giver, g, giver, slot, giver).wait_recv()
        send_o[giver, slot], send_l[giver, slot] = owner_block(recv_q[giver, slot], g, slot == 2)
        return (
            o_copy(giver, slot, owner, g, giver),
            l_copy(giver, slot, owner, g, giver),
        )

    def serve_near(step, carry):
        giver = xor(me, step, n)
        for slot in range(2):
            for copy in serve(giver, slot):
                copy.start()
        return carry

    def serve_far(step, carry):
        for copy in serve(xor(me, step, n), 0):
            copy.start()
        return carry

    def serve_mate(step, carry):
        for copy in serve(xor(me, step, n), 2):
            copy.start()
        return carry

    for g in range(kv_heads):
        recv_o[me, g], recv_l[me, g] = owner_block(send_q[me, g], g)

    row_id = lax.broadcasted_iota(jnp.int32, (tok, tok), 0)
    col_id = lax.broadcasted_iota(jnp.int32, (tok, tok), 1)
    begin = jnp.zeros((tok, tok), jnp.int32)
    for k in range(1, resp):
        begin = jnp.where(row_id >= starts[k], starts[k], begin)
    allowed = (col_id >= begin) & (col_id <= row_id)
    lane_tok = lax.broadcasted_iota(jnp.int32, (tok, LANES), 1)

    local_log = jnp.zeros((tok, LANES), F32)
    for h in range(heads):
        g = h // per_kv
        scores = nt_dot(q_ref[:, h * HD : (h + 1) * HD], rk_ref[:, g * HD : (g + 1) * HD])
        scores = jnp.where(allowed, scores, -1e30)
        highest = jnp.max(scores, axis=1, keepdims=True)
        weights = jnp.exp2((scores - highest) * power).astype(BF16)
        both = jnp.dot(weights, rv_ext[g], preferred_element_type=F32)
        total = both[:, HD:]
        local_o[h] = both[:, :HD] / total
        local_log = jnp.where(lane_tok == h, highest * power + jnp.log2(total), local_log)
    local_l[...] = local_log

    lax.fori_loop(1, half, serve_near, 0)
    lax.fori_loop(half, n, serve_far, 0)
    for which in range(2):
        kv_copy(which).wait_recv()
    v_ext[kv_heads] = jnp.concatenate([far_kv[1], jnp.ones((pk_ref.shape[0], HD), BF16)], axis=1)
    lax.fori_loop(1, half, serve_mate, 0)
    recv_o[mate, 1], recv_l[mate, 1] = owner_block(send_q[mate, 1], 1, True)

    column = lax.broadcasted_iota(jnp.int32, (8, n * LEN_MOST), 1)
    targets = [jnp.full((8, n * LEN_MOST), -1, jnp.int32) for _ in range(shards)]
    for d in range(n):
        first, live, which = placed(d)
        place = column - d * LEN_MOST
        here = (place >= 0) & (place < live)
        for j in range(shards):
            targets[j] = jnp.where(here & (which == j), place + first, targets[j])
    token_row = lax.broadcasted_iota(jnp.int32, (tok, n * LEN_MOST), 0)
    chosen = [
        (token_row == jnp.broadcast_to(t[0:1, :], (tok, n * LEN_MOST))).astype(F32).astype(BF16)
        for t in targets
    ]
    chosen = jnp.concatenate(chosen, axis=0)

    def receive(d, g):
        o_copy(d, g, d, g, d).wait_recv()
        l_copy(d, g, d, g, d).wait_recv()

    def receive_near(step, carry):
        peer = xor(me, step, n)
        receive(peer, 0)
        receive(peer, 1)
        receive(xor(peer, half, n), 1)
        return carry

    def receive_far(step, carry):
        receive(xor(me, step, n), 0)
        return carry

    lax.fori_loop(half, n, receive_far, 0)
    lax.fori_loop(1, half, receive_near, 0)

    log_rows = []
    for d in range(n):
        packed = recv_l[d, 0] + recv_l[d, 1]
        for k in range(GROUPS_OF_8):
            log_rows.append(pltpu.roll(packed, LANES - k * heads, 1) if k else packed)
    log_all = jnp.concatenate(log_rows, axis=0)
    high = log_all.astype(BF16)
    rest = log_all - high.astype(F32)
    middle = rest.astype(BF16)
    low = (rest - middle.astype(F32)).astype(BF16)
    logs = jnp.dot(chosen, high, preferred_element_type=F32)
    logs = logs + jnp.dot(chosen, middle, preferred_element_type=F32)
    logs = logs + jnp.dot(chosen, low, preferred_element_type=F32)
    parts_log = [local_l[...]] + [logs[j * tok : (j + 1) * tok] for j in range(shards)]
    highest = functools.reduce(jnp.maximum, parts_log)
    shares = [jnp.exp2(part - highest) for part in parts_log]
    inverse = 1.0 / functools.reduce(jnp.add, shares)
    shares = [share * inverse for share in shares]

    for g in range(kv_heads):
        wide = [recv_o[d, g].astype(F32) for d in range(n)]
        for h in range(per_kv):
            head = g * per_kv + h
            stacked = jnp.concatenate(
                [w[h * LEN_MOST : (h + 1) * LEN_MOST] for w in wide], axis=0
            ).astype(BF16)
            taken = jnp.dot(chosen, stacked, preferred_element_type=F32)
            blended = shares[0][:, head : head + 1] * local_o[head]
            for j in range(shards):
                blended = blended + (
                    shares[j + 1][:, head : head + 1] * taken[j * tok : (j + 1) * tok]
                )
            out_ref[:, head * HD : (head + 1) * HD] = blended.astype(BF16)

    def finish_near(step, carry):
        peer = xor(me, step, n)
        q_copy(peer, 0, me, 0, peer).wait_send()
        q_copy(peer, 1, me, 1, peer).wait_send()
        q_copy(xor(peer, half, n), 1, me, 2, peer).wait_send()
        for slot in range(3):
            o_copy(peer, slot, me, 0, peer).wait_send()
            l_copy(peer, slot, me, 0, peer).wait_send()
        return carry

    def finish_far(step, carry):
        peer = xor(me, step, n)
        q_copy(peer, 0, me, 0, peer).wait_send()
        o_copy(peer, 0, me, 0, peer).wait_send()
        l_copy(peer, 0, me, 0, peer).wait_send()
        return carry

    for which in range(2):
        kv_copy(which).wait_send()
    lax.fori_loop(1, half, finish_near, 0)
    lax.fori_loop(half, n, finish_far, 0)


def per_device(
    queries,
    resp_keys,
    resp_values,
    prompt_keys,
    prompt_values,
    response_prompt,
    response_lengths,
    shard_order,
):
    n = lax.axis_size("seq")
    tok = queries.shape[0]
    kv_heads = resp_keys.shape[1] // HD
    heads = queries.shape[1] // HD
    rows = heads // kv_heads * LEN_MOST
    keys = prompt_keys.shape[0]
    block = (n, kv_heads, rows, HD)
    slots = (n, 3, rows, HD)
    smem = pl.BlockSpec(memory_space=pltpu.SMEM)
    vmem = pl.BlockSpec(memory_space=pltpu.VMEM)
    return pl.pallas_call(
        functools.partial(kernel, n),
        out_shape=jax.ShapeDtypeStruct(queries.shape, BF16),
        in_specs=[smem] * 3 + [vmem] * 5,
        out_specs=vmem,
        scratch_shapes=[
            pltpu.VMEM(block, BF16),
            pltpu.VMEM(slots, BF16),
            pltpu.VMEM(slots, BF16),
            pltpu.VMEM(block, BF16),
            pltpu.VMEM((n, 3, 8, LANES), F32),
            pltpu.VMEM((n, kv_heads, 8, LANES), F32),
            pltpu.VMEM((2, keys, HD), BF16),
            pltpu.VMEM((kv_heads + 1, keys, 2 * HD), BF16),
            pltpu.VMEM((kv_heads, tok, 2 * HD), BF16),
            pltpu.VMEM((heads, tok, HD), F32),
            pltpu.VMEM((tok, LANES), F32),
            pltpu.SemaphoreType.DMA((n, kv_heads)),
            pltpu.SemaphoreType.DMA((n, 3)),
            pltpu.SemaphoreType.DMA((n, 3)),
            pltpu.SemaphoreType.DMA((n, kv_heads)),
            pltpu.SemaphoreType.DMA((n, 3)),
            pltpu.SemaphoreType.DMA((n, kv_heads)),
            pltpu.SemaphoreType.DMA((2,)),
            pltpu.SemaphoreType.DMA((2,)),
        ],
        compiler_params=pltpu.CompilerParams(
            collective_id=0, has_side_effects=True, vmem_limit_bytes=56 * 1024 * 1024
        ),
    )(
        shard_order,
        response_prompt,
        response_lengths,
        queries,
        resp_keys,
        resp_values,
        prompt_keys,
        prompt_values,
    )


def solution(mesh):
    return jax.shard_map(
        per_device,
        mesh=mesh,
        in_specs=(
            P(("groups", "seq"), "tensor"),
            P(("groups", "seq"), "tensor"),
            P(("groups", "seq"), "tensor"),
            P(("groups", "seq"), "tensor"),
            P(("groups", "seq"), "tensor"),
            P(("groups", "seq"), None),
            P(("groups", "seq"), None),
            P("groups"),
        ),
        out_specs=P(("groups", "seq"), "tensor"),
        check_vma=False,
    )
```

```python
import functools
import math

import jax
import jax.numpy as jnp
from jax import lax
from jax.experimental import pallas as pl
from jax.experimental.pallas import tpu as pltpu
from jax.sharding import PartitionSpec as P

HD = 128
PROMPTS = 4
LEN_MOST = 40
LANES = 128
GROUPS_OF_8 = LEN_MOST // 8
LOG2E = 1.4426950408889634
MESH = pl.DeviceIdType.MESH

F32 = jnp.float32
BF16 = jnp.bfloat16


def xor(a, b, n):
    total = 0
    bit = 1
    while bit < n:
        total = total + bit * (((a // bit) % 2 + (b // bit) % 2) % 2)
        bit *= 2
    return total


def nt_dot(a, b):
    return lax.dot_general(a, b, (((1,), (1,)), ((), ())), preferred_element_type=F32)


def kernel(
    n,
    order_ref,
    prompt_ref,
    len_ref,
    q_hbm,
    rk_hbm,
    rv_hbm,
    pk_hbm,
    pv_hbm,
    out_ref,
    q_ref,
    rk_ref,
    rv_ref,
    pk_ref,
    pv_ref,
    load_sem,
    send_q,
    recv_q,
    send_o,
    recv_o,
    send_l,
    recv_l,
    far_kv,
    v_ext,
    rv_ext,
    local_o,
    local_l,
    q_send_sem,
    q_recv_sem,
    o_send_sem,
    o_recv_sem,
    l_send_sem,
    l_recv_sem,
    kv_send_sem,
    kv_recv_sem,
):
    me = lax.axis_index("seq")
    half = n // 2
    mate = xor(me, half, n)
    shards = n // PROMPTS
    tok = q_ref.shape[0]
    kv_heads = rk_ref.shape[1] // HD
    heads = q_ref.shape[1] // HD
    per_kv = heads // kv_heads
    resp = prompt_ref.shape[1]
    power = LOG2E / math.sqrt(HD)

    barrier = pltpu.get_barrier_semaphore()

    def greet(step, carry):
        pl.semaphore_signal(
            barrier, inc=1, device_id={"seq": xor(me, step, n)}, device_id_type=MESH
        )
        return carry

    lax.fori_loop(1, n, greet, 0)

    loads = [
        pltpu.make_async_copy(source, target, load_sem.at[i])
        for i, (source, target) in enumerate(
            (
                (q_hbm, q_ref),
                (pk_hbm, pk_ref),
                (pv_hbm, pv_ref),
                (rk_hbm, rk_ref),
                (rv_hbm, rv_ref),
            )
        )
    ]
    for load in loads:
        load.start()

    lengths = [len_ref[0, k] for k in range(resp)]
    prompts = [prompt_ref[0, k] for k in range(resp)]
    starts = [jnp.int32(0)]
    for k in range(resp - 1):
        starts.append(starts[-1] + lengths[k])

    def placed(d):
        rank = order_ref[d]
        first = jnp.int32(0)
        live = jnp.int32(0)
        which = jnp.int32(0)
        for k in range(resp):
            low = prompts[k] * shards
            hit = (rank >= low) & (rank < low + shards)
            first = jnp.where(hit, starts[k], first)
            live = jnp.where(hit, lengths[k], live)
            which = jnp.where(hit, rank - low, which)
        return first, live, which

    slot_id = lax.broadcasted_iota(jnp.int32, (LEN_MOST, tok), 0)
    token_id = lax.broadcasted_iota(jnp.int32, (LEN_MOST, tok), 1)

    def gather_block(d):
        first, live, _ = placed(d)
        chosen = ((token_id == first + slot_id) & (slot_id < live)).astype(F32).astype(BF16)
        picked = jnp.dot(chosen, q_ref[...], preferred_element_type=F32)
        for g in range(kv_heads):
            parts = [
                picked[:, (g * per_kv + h) * HD : (g * per_kv + h + 1) * HD] for h in range(per_kv)
            ]
            send_q[d, g] = jnp.concatenate(parts, axis=0).astype(BF16)

    def q_copy(d, g, giver, slot, peer):
        return pltpu.make_async_remote_copy(
            src_ref=send_q.at[d, g],
            dst_ref=recv_q.at[giver, slot],
            send_sem=q_send_sem.at[d, g],
            recv_sem=q_recv_sem.at[giver, slot],
            device_id={"seq": peer},
            device_id_type=MESH,
        )

    def o_copy(giver, slot, d, g, peer):
        return pltpu.make_async_remote_copy(
            src_ref=send_o.at[giver, slot],
            dst_ref=recv_o.at[d, g],
            send_sem=o_send_sem.at[giver, slot],
            recv_sem=o_recv_sem.at[d, g],
            device_id={"seq": peer},
            device_id_type=MESH,
        )

    def l_copy(giver, slot, d, g, peer):
        return pltpu.make_async_remote_copy(
            src_ref=send_l.at[giver, slot],
            dst_ref=recv_l.at[d, g],
            send_sem=l_send_sem.at[giver, slot],
            recv_sem=l_recv_sem.at[d, g],
            device_id={"seq": peer},
            device_id_type=MESH,
        )

    def kv_copy(which):
        source = (pk_hbm, pv_hbm)[which]
        return pltpu.make_async_remote_copy(
            src_ref=source.at[:, pl.ds(HD, HD)],
            dst_ref=far_kv.at[which],
            send_sem=kv_send_sem.at[which],
            recv_sem=kv_recv_sem.at[which],
            device_id={"seq": mate},
            device_id_type=MESH,
        )

    def gather_far(step, carry):
        gather_block(xor(me, step, n))
        return carry

    def send_far(step, carry):
        peer = xor(me, step, n)
        q_copy(peer, 0, me, 0, peer).start()
        return carry

    def send_near(step, carry):
        peer = xor(me, step, n)
        gather_block(peer)
        q_copy(peer, 0, me, 0, peer).start()
        q_copy(peer, 1, me, 1, peer).start()
        q_copy(xor(peer, half, n), 1, me, 2, peer).start()
        return carry

    loads[0].wait()
    lax.fori_loop(half, n, gather_far, 0)
    pl.semaphore_wait(barrier, n - 1)
    kv_copy(0).start()
    kv_copy(1).start()
    lax.fori_loop(half, n, send_far, 0)
    lax.fori_loop(1, half, send_near, 0)
    gather_block(me)
    for load in loads[1:]:
        load.wait()

    ones = jnp.ones((pk_ref.shape[0], HD), BF16)
    for g in range(kv_heads):
        v_ext[g] = jnp.concatenate([pv_ref[:, g * HD : (g + 1) * HD], ones], axis=1)
    ones = jnp.ones((tok, HD), BF16)
    for g in range(kv_heads):
        rv_ext[g] = jnp.concatenate([rv_ref[:, g * HD : (g + 1) * HD], ones], axis=1)

    lane8 = lax.broadcasted_iota(jnp.int32, (8, LANES), 1)

    def owner_block(q_block, g, far=False):
        keys = far_kv[0] if far else pk_ref[:, g * HD : (g + 1) * HD]
        scores = nt_dot(q_block, keys)
        highest = jnp.max(scores, axis=1, keepdims=True)
        weights = jnp.exp2((scores - highest) * power).astype(BF16)
        both = jnp.dot(weights, v_ext[kv_heads if far else g], preferred_element_type=F32)
        total = both[:, HD:]
        logs = highest * power + jnp.log2(total)
        packed = jnp.zeros((8, LANES), F32)
        for h in range(per_kv):
            for k in range(GROUPS_OF_8):
                row = h * LEN_MOST + k * 8
                packed = jnp.where(
                    lane8 == k * heads + g * per_kv + h, logs[row : row + 8, :], packed
                )
        return (both[:, :HD] / total).astype(BF16), packed

    def serve(giver, slot):
        g = min(slot, 1)
        owner = mate if slot == 2 else me
        q_copy(giver, g, giver, slot, giver).wait_recv()
        send_o[giver, slot], send_l[giver, slot] = owner_block(recv_q[giver, slot], g, slot == 2)
        return (
            o_copy(giver, slot, owner, g, giver),
            l_copy(giver, slot, owner, g, giver),
        )

    def serve_near(step, carry):
        giver = xor(me, step, n)
        for slot in range(2):
            for copy in serve(giver, slot):
                copy.start()
        return carry

    def serve_far(step, carry):
        for copy in serve(xor(me, step, n), 0):
            copy.start()
        return carry

    def serve_mate(step, carry):
        for copy in serve(xor(me, step, n), 2):
            copy.start()
        return carry

    for g in range(kv_heads):
        recv_o[me, g], recv_l[me, g] = owner_block(send_q[me, g], g)

    row_id = lax.broadcasted_iota(jnp.int32, (tok, tok), 0)
    col_id = lax.broadcasted_iota(jnp.int32, (tok, tok), 1)
    begin = jnp.zeros((tok, tok), jnp.int32)
    for k in range(1, resp):
        begin = jnp.where(row_id >= starts[k], starts[k], begin)
    allowed = (col_id >= begin) & (col_id <= row_id)
    lane_tok = lax.broadcasted_iota(jnp.int32, (tok, LANES), 1)

    local_log = jnp.zeros((tok, LANES), F32)
    for h in range(heads):
        g = h // per_kv
        scores = nt_dot(q_ref[:, h * HD : (h + 1) * HD], rk_ref[:, g * HD : (g + 1) * HD])
        scores = jnp.where(allowed, scores, -1e30)
        highest = jnp.max(scores, axis=1, keepdims=True)
        weights = jnp.exp2((scores - highest) * power).astype(BF16)
        both = jnp.dot(weights, rv_ext[g], preferred_element_type=F32)
        total = both[:, HD:]
        local_o[h] = both[:, :HD] / total
        local_log = jnp.where(lane_tok == h, highest * power + jnp.log2(total), local_log)
    local_l[...] = local_log

    lax.fori_loop(1, half, serve_near, 0)
    lax.fori_loop(half, n, serve_far, 0)
    for which in range(2):
        kv_copy(which).wait_recv()
    v_ext[kv_heads] = jnp.concatenate([far_kv[1], jnp.ones((pk_ref.shape[0], HD), BF16)], axis=1)
    lax.fori_loop(1, half, serve_mate, 0)
    recv_o[mate, 1], recv_l[mate, 1] = owner_block(send_q[mate, 1], 1, True)

    column = lax.broadcasted_iota(jnp.int32, (8, n * LEN_MOST), 1)
    targets = [jnp.full((8, n * LEN_MOST), -1, jnp.int32) for _ in range(shards)]
    for d in range(n):
        first, live, which = placed(d)
        place = column - d * LEN_MOST
        here = (place >= 0) & (place < live)
        for j in range(shards):
            targets[j] = jnp.where(here & (which == j), place + first, targets[j])
    token_row = lax.broadcasted_iota(jnp.int32, (tok, n * LEN_MOST), 0)
    chosen = [
        (token_row == jnp.broadcast_to(t[0:1, :], (tok, n * LEN_MOST))).astype(F32).astype(BF16)
        for t in targets
    ]
    chosen = jnp.concatenate(chosen, axis=0)

    def receive(d, g):
        o_copy(d, g, d, g, d).wait_recv()
        l_copy(d, g, d, g, d).wait_recv()

    def receive_near(step, carry):
        peer = xor(me, step, n)
        receive(peer, 0)
        receive(peer, 1)
        receive(xor(peer, half, n), 1)
        return carry

    def receive_far(step, carry):
        receive(xor(me, step, n), 0)
        return carry

    lax.fori_loop(half, n, receive_far, 0)
    lax.fori_loop(1, half, receive_near, 0)

    log_rows = []
    for d in range(n):
        packed = recv_l[d, 0] + recv_l[d, 1]
        for k in range(GROUPS_OF_8):
            log_rows.append(pltpu.roll(packed, LANES - k * heads, 1) if k else packed)
    log_all = jnp.concatenate(log_rows, axis=0)
    high = log_all.astype(BF16)
    rest = log_all - high.astype(F32)
    middle = rest.astype(BF16)
    low = (rest - middle.astype(F32)).astype(BF16)
    logs = jnp.dot(chosen, high, preferred_element_type=F32)
    logs = logs + jnp.dot(chosen, middle, preferred_element_type=F32)
    logs = logs + jnp.dot(chosen, low, preferred_element_type=F32)
    parts_log = [local_l[...]] + [logs[j * tok : (j + 1) * tok] for j in range(shards)]
    highest = functools.reduce(jnp.maximum, parts_log)
    shares = [jnp.exp2(part - highest) for part in parts_log]
    inverse = 1.0 / functools.reduce(jnp.add, shares)
    shares = [share * inverse for share in shares]

    for g in range(kv_heads):
        wide = [recv_o[d, g].astype(F32) for d in range(n)]
        for h in range(per_kv):
            head = g * per_kv + h
            stacked = jnp.concatenate(
                [w[h * LEN_MOST : (h + 1) * LEN_MOST] for w in wide], axis=0
            ).astype(BF16)
            taken = jnp.dot(chosen, stacked, preferred_element_type=F32)
            blended = shares[0][:, head : head + 1] * local_o[head]
            for j in range(shards):
                blended = blended + (
                    shares[j + 1][:, head : head + 1] * taken[j * tok : (j + 1) * tok]
                )
            out_ref[:, head * HD : (head + 1) * HD] = blended.astype(BF16)

    def finish_near(step, carry):
        peer = xor(me, step, n)
        q_copy(peer, 0, me, 0, peer).wait_send()
        q_copy(peer, 1, me, 1, peer).wait_send()
        q_copy(xor(peer, half, n), 1, me, 2, peer).wait_send()
        for slot in range(3):
            o_copy(peer, slot, me, 0, peer).wait_send()
            l_copy(peer, slot, me, 0, peer).wait_send()
        return carry

    def finish_far(step, carry):
        peer = xor(me, step, n)
        q_copy(peer, 0, me, 0, peer).wait_send()
        o_copy(peer, 0, me, 0, peer).wait_send()
        l_copy(peer, 0, me, 0, peer).wait_send()
        return carry

    for which in range(2):
        kv_copy(which).wait_send()
    lax.fori_loop(1, half, finish_near, 0)
    lax.fori_loop(half, n, finish_far, 0)


def per_device(
    queries,
    resp_keys,
    resp_values,
    prompt_keys,
    prompt_values,
    response_prompt,
    response_lengths,
    shard_order,
):
    n = lax.axis_size("seq")
    tok = queries.shape[0]
    kv_heads = resp_keys.shape[1] // HD
    heads = queries.shape[1] // HD
    rows = heads // kv_heads * LEN_MOST
    keys = prompt_keys.shape[0]
    block = (n, kv_heads, rows, HD)
    slots = (n, 3, rows, HD)
    smem = pl.BlockSpec(memory_space=pltpu.SMEM)
    vmem = pl.BlockSpec(memory_space=pltpu.VMEM)
    return pl.pallas_call(
        functools.partial(kernel, n),
        out_shape=jax.ShapeDtypeStruct(queries.shape, BF16),
        in_specs=[smem] * 3 + [pl.BlockSpec(memory_space=pltpu.HBM)] * 5,
        out_specs=vmem,
        scratch_shapes=[
            pltpu.VMEM(queries.shape, BF16),
            pltpu.VMEM(resp_keys.shape, BF16),
            pltpu.VMEM(resp_values.shape, BF16),
            pltpu.VMEM(prompt_keys.shape, BF16),
            pltpu.VMEM(prompt_values.shape, BF16),
            pltpu.SemaphoreType.DMA((5,)),
            pltpu.VMEM(block, BF16),
            pltpu.VMEM(slots, BF16),
            pltpu.VMEM(slots, BF16),
            pltpu.VMEM(block, BF16),
            pltpu.VMEM((n, 3, 8, LANES), F32),
            pltpu.VMEM((n, kv_heads, 8, LANES), F32),
            pltpu.VMEM((2, keys, HD), BF16),
            pltpu.VMEM((kv_heads + 1, keys, 2 * HD), BF16),
            pltpu.VMEM((kv_heads, tok, 2 * HD), BF16),
            pltpu.VMEM((heads, tok, HD), F32),
            pltpu.VMEM((tok, LANES), F32),
            pltpu.SemaphoreType.DMA((n, kv_heads)),
            pltpu.SemaphoreType.DMA((n, 3)),
            pltpu.SemaphoreType.DMA((n, 3)),
            pltpu.SemaphoreType.DMA((n, kv_heads)),
            pltpu.SemaphoreType.DMA((n, 3)),
            pltpu.SemaphoreType.DMA((n, kv_heads)),
            pltpu.SemaphoreType.DMA((2,)),
            pltpu.SemaphoreType.DMA((2,)),
        ],
        compiler_params=pltpu.CompilerParams(
            collective_id=0, has_side_effects=True, vmem_limit_bytes=56 * 1024 * 1024
        ),
    )(
        shard_order,
        response_prompt.reshape(1, -1),
        response_lengths,
        queries,
        resp_keys,
        resp_values,
        prompt_keys,
        prompt_values,
    )


def solution(mesh):
    return jax.shard_map(
        per_device,
        mesh=mesh,
        in_specs=(
            P(("groups", "seq"), "tensor"),
            P(("groups", "seq"), "tensor"),
            P(("groups", "seq"), "tensor"),
            P(("groups", "seq"), "tensor"),
            P(("groups", "seq"), "tensor"),
            P(("groups", "seq"), None),
            P(("groups", "seq"), None),
            P("groups"),
        ),
        out_specs=P(("groups", "seq"), "tensor"),
        check_vma=False,
    )
```
